256 devices in a mesh: member: 32 (over y, z), patch: 4 (over x), level: 2 (over core).
Axes of the slice: x: 4, y: 4, z: 8, core: 2. Of those that a mesh axis runs over, the one named last changes fastest.
Arguments:
- ensemble: bfloat16 [256, 4, 32, 2, 12, 1024], P('member', 'patch', None, 'level'), may hold values from -6 to 6
- observations: float32 [4, 32, 2, 128], P('patch', 'member'), may hold values from -9 to 9
- precision: float32 [4, 32, 2, 128], P('patch', 'member'), may hold values from 0.25 to 4
- valid_count: int32 [4, 32, 2], P('patch', 'member'), may hold values from 16 to 128, as said below
- position: int32 [4, 32, 2, 128], P('patch', 'member'), may hold values from 0 to 12287
- level_kernel: float32 [2, 12], P('level'), may hold values from -4 to 4
- listed_blocks: int32 [4, 32, 8], P('patch', 'member'), may hold values from 0 to 17, as said below
Outputs:
- analysis: bfloat16 [256, 4, 32, 2, 12, 1024], P('member', 'patch', None, 'level')
The draws below stay inside these ranges and needn't reach their ends.
Inputs may be any that keep to these rules, and one draw needn't show every extreme that they name: `valid_count`: the valid observations of a block are its first slots; some block is full and some holds 16. `listed_blocks`: the entries of one patch are distinct, include both of the patch's own blocks (candidates 8 and 9), and name only patches inside the grid.
All inputs are finite; a program needn't handle non-finite values.
Results may differ from the reference program's by a relative error of at most 0.0082.
Values may be sent and summed in bfloat16 or wider, within the bound.
No kernel may reach another device: no remote copies, remote signals or barrier semaphores. Data moves between devices by JAX's collectives and lax.ppermute only.
A program may use at most 128 MiB of HBM per device.

```python
import math
import jax
import jax.numpy as jnp
from jax import lax

MEMBERS = 256
VARIABLES = 12
COLUMNS = 1024
SLOTS = 128
OWN_BLOCKS = 2
LISTED = 8
SWEEPS = 6
LEVELS = 2
PATCH_ROWS = 4
PATCH_COLS = 32


def draw_valid_count(key, part):
    key = jax.random.fold_in(key, 5)
    counts = jax.random.randint(key, (PATCH_ROWS, PATCH_COLS, OWN_BLOCKS), SLOTS // 8, SLOTS + 1, dtype=jnp.int32)
    counts = counts.at[0, 0, 0].set(SLOTS)
    return counts.at[PATCH_ROWS - 1, PATCH_COLS - 1, OWN_BLOCKS - 1].set(SLOTS // 8)


def draw_listed_blocks(key, part):
    key = jax.random.fold_in(key, 9)
    total = 9 * OWN_BLOCKS
    grid_rows = jnp.arange(PATCH_ROWS, dtype=jnp.int32)[:, None, None]
    grid_cols = jnp.arange(PATCH_COLS, dtype=jnp.int32)[None, :, None]
    choices_all = jnp.arange(total, dtype=jnp.int32)[None, None, :]
    stepped = choices_all // OWN_BLOCKS
    row_shift = stepped // 3 - 1
    col_shift = stepped % 3 - 1
    inside = (grid_rows + row_shift >= 0) & (grid_rows + row_shift < PATCH_ROWS)
    inside = inside & (grid_cols + col_shift >= 0) & (grid_cols + col_shift < PATCH_COLS)
    centred = (row_shift == 0) & (col_shift == 0)
    noise = jax.random.randint(key, (PATCH_ROWS, PATCH_COLS, total), 0, 1 << 20, dtype=jnp.int32)
    scores = noise * 64 + choices_all + inside.astype(jnp.int32) * (1 << 27) + centred.astype(jnp.int32) * (1 << 28)
    return jax.lax.top_k(scores, LISTED)[1].astype(jnp.int32)


def plant(values, key, low, top_value):
    place = [jax.random.randint(jax.random.fold_in(key, axis), (), 0, length) for axis, length in enumerate(values.shape)]
    longest = values.shape.index(max(values.shape))
    neighbour = place[:longest] + [(place[longest] + 1) % values.shape[longest]] + place[longest + 1:]
    return values.at[tuple(place)].set(low).at[tuple(neighbour)].set(top_value)


def block_scale(rng, dims, shards, low, high):
    def one(dim, parts):
        heights = jax.random.uniform(jax.random.fold_in(jax.random.fold_in(rng, 6), dim), (parts,), jnp.float32, low / len(shards), high / len(shards))
        return jnp.repeat(jnp.exp(heights), dims[dim] // parts).reshape((-1,) + (1,) * (len(dims) - dim - 1))

    gain = one(*shards[0])
    for cut in shards[1:]:
        gain = gain * one(*cut)
    return gain


def normal_values(own_key, dims, spread, most, shards=(), held_as=jnp.bfloat16):
    entries = spread * jax.random.normal(own_key, dims, jnp.float32)
    if shards:
        entries = entries * block_scale(own_key, dims, shards, -0.22, 0.18)
    return jnp.clip(entries, -most, most).astype(held_as)


def setup_inputs(seed: int = 0) -> dict:
    splits = jax.random.split(jax.random.key(seed), 8)
    ensemble = normal_values(splits[0], (MEMBERS, PATCH_ROWS, PATCH_COLS, LEVELS, VARIABLES, COLUMNS), 1.0, 6.0, ((0, 32), (1, 4), (3, 2)))
    observations = normal_values(splits[1], (PATCH_ROWS, PATCH_COLS, OWN_BLOCKS, SLOTS), 1.5, 9.0, ((0, 4), (1, 32)), jnp.float32)
    precision = jnp.clip(jnp.exp(math.log(4.0) - 2.7725887 * jax.random.uniform(splits[2], (PATCH_ROWS, PATCH_COLS, OWN_BLOCKS, SLOTS), jnp.float32) ** block_scale(splits[2], (PATCH_ROWS, PATCH_COLS, OWN_BLOCKS, SLOTS), ((0, 4), (1, 32)), -0.2, 0.2)), 0.25, 4.0)
    valid_count = draw_valid_count(jax.random.fold_in(splits[7], 71), 0)
    position = plant(jax.random.randint(splits[4], (PATCH_ROWS, PATCH_COLS, OWN_BLOCKS, SLOTS), 0, VARIABLES * COLUMNS), jax.random.fold_in(splits[4], 1), 0, (VARIABLES * COLUMNS) - 1).astype(jnp.int32)
    level_kernel = normal_values(splits[5], (LEVELS, VARIABLES), 1.0, 4.0, ((0, 2),), jnp.float32)
    listed_blocks = draw_listed_blocks(jax.random.fold_in(splits[7], 71), 0)
    return {"ensemble": ensemble, "observations": observations, "precision": precision, "valid_count": valid_count, "position": position, "level_kernel": level_kernel, "listed_blocks": listed_blocks}


exact_precision = lax.Precision.HIGHEST

def taper_of(listed):
    stepped = listed // OWN_BLOCKS
    moved = jnp.abs(stepped // 3 - 1) + jnp.abs(stepped % 3 - 1)
    return jnp.where(moved == 0, 1.0, jnp.where(moved == 1, 0.6, 0.35)).astype(jnp.float32)

def analyse_patch(candidates, pairs, listed, fields):
    members = candidates.shape[0]
    chosen = jnp.take(candidates, listed, axis=1).reshape(members, LISTED * SLOTS)
    picked = jnp.take(pairs, listed, axis=1)
    tapering = taper_of(listed)
    widened = lax.optimization_barrier(chosen).astype(jnp.float32)
    centre = lax.optimization_barrier(jnp.mean(widened, axis=0))
    obs_pert = (widened - centre).astype(jnp.bfloat16)
    weight = (picked[1] * tapering[:, None]).reshape(LISTED * SLOTS)
    innovation = picked[0].reshape(LISTED * SLOTS) - centre
    pert_wide = lax.optimization_barrier(obs_pert).astype(jnp.float32)
    scaled = (pert_wide * jnp.sqrt(weight)).astype(jnp.bfloat16)
    identity = jnp.eye(members, dtype=jnp.float32)
    system = lax.dot_general(scaled, scaled, (((1,), (1,)), ((), ())), preferred_element_type=jnp.float32)
    system = system + (members - 1) / 1.1 * identity
    scaling = jnp.sqrt(jnp.sum(system * system))
    iterate = system / scaling
    inverse_root = identity
    for iteration in range(SWEEPS):
        middle = 1.5 * identity - 0.5 * jnp.dot(inverse_root, iterate, precision=exact_precision)
        iterate = jnp.dot(iterate, middle, precision=exact_precision)
        inverse_root = jnp.dot(middle, inverse_root, precision=exact_precision)
    forcing = jnp.dot(pert_wide, weight * innovation, precision=exact_precision)
    inner = jnp.dot(inverse_root, forcing, precision=exact_precision)
    mean_weight = jnp.dot(inverse_root, inner, precision=exact_precision) / scaling
    weights = (jnp.sqrt((members - 1) / scaling) * inverse_root + mean_weight[:, None]).astype(jnp.bfloat16)
    field_mean = lax.optimization_barrier(jnp.mean(fields, axis=0, dtype=jnp.float32))
    field_pert = (fields - field_mean).astype(jnp.bfloat16)
    updated = lax.dot_general(weights, field_pert, (((0,), (0,)), ((), ())), preferred_element_type=jnp.float32)
    return (updated + field_mean).astype(jnp.bfloat16)

def reference(ensemble, observations, precision, valid_count, position, level_kernel, listed_blocks):
    members = ensemble.shape[0]
    patches = PATCH_ROWS * PATCH_COLS
    zero = jnp.zeros((), jnp.int32)

    def patch_fields(number):
        grid_row = number // PATCH_COLS
        grid_col = number % PATCH_COLS
        block = lax.dynamic_index_in_dim(ensemble, grid_row, 1, keepdims=False)
        block = lax.dynamic_index_in_dim(block, grid_col, 1, keepdims=False)
        return block
    flat_position = position.reshape(patches, OWN_BLOCKS * SLOTS)

    def observe(number):
        fields = patch_fields(number).reshape(members, LEVELS, VARIABLES * COLUMNS)
        where_flat = flat_position[number]
        picked = fields[:, :, where_flat].astype(jnp.float32)
        factor = level_kernel[:, where_flat // COLUMNS]
        return lax.optimization_barrier(jnp.sum(picked * factor[None], axis=1)).astype(jnp.bfloat16)
    numbers = jnp.arange(patches, dtype=jnp.int32)
    equivalent = lax.map(observe, numbers)
    equivalent = equivalent.reshape(PATCH_ROWS, PATCH_COLS, members, OWN_BLOCKS, SLOTS)
    padded_equiv = jnp.pad(equivalent, ((1, 1), (1, 1), (0, 0), (0, 0), (0, 0)))
    slot_index = lax.broadcasted_iota(jnp.int32, precision.shape, 3)
    precision_used = jnp.where(slot_index < valid_count[..., None], precision, 0.0)
    pairs_all = jnp.stack([observations, precision_used], axis=2)
    padded_pairs = jnp.pad(pairs_all, ((1, 1), (1, 1), (0, 0), (0, 0), (0, 0)))
    flat_listed = listed_blocks.reshape(patches, LISTED)

    def analyse(number):
        grid_row = number // PATCH_COLS
        grid_col = number % PATCH_COLS
        near = lax.dynamic_slice(padded_equiv, (grid_row, grid_col, zero, zero, zero), (3, 3, members, OWN_BLOCKS, SLOTS))
        near = near.transpose(2, 0, 1, 3, 4).reshape(members, 9 * OWN_BLOCKS, SLOTS)
        near_pairs = lax.dynamic_slice(padded_pairs, (grid_row, grid_col, zero, zero, zero), (3, 3, 2, OWN_BLOCKS, SLOTS))
        near_pairs = near_pairs.transpose(2, 0, 1, 3, 4).reshape(2, 9 * OWN_BLOCKS, SLOTS)
        fields = patch_fields(number).reshape(members, LEVELS * VARIABLES * COLUMNS)
        return analyse_patch(near, near_pairs, flat_listed[number], fields)
    result = lax.map(analyse, numbers)
    result = result.reshape(PATCH_ROWS, PATCH_COLS, members, LEVELS, VARIABLES, COLUMNS)
    return result.transpose(2, 0, 1, 3, 4, 5)
```

```python
import jax
import jax.numpy as jnp
from jax import lax
from jax.experimental import pallas as pl
from jax.experimental.pallas import tpu as pltpu
from jax.sharding import PartitionSpec as P

VARIABLES = 12
COLUMNS = 1024
SLOTS = 128
OWN_BLOCKS = 2
LISTED = 8
SWEEPS = 6
FIRST = 2

exact_precision = lax.Precision.HIGHEST
barrier = lax.optimization_barrier


def exchange(cells):
    return lax.all_to_all(cells, "member", split_axis=0, concat_axis=0, tiled=True)


def row_halo(cells):
    count = lax.axis_size("patch")
    above = lax.ppermute(cells, "patch", [(i, i + 1) for i in range(count - 1)])
    below = lax.ppermute(cells, "patch", [(i + 1, i) for i in range(count - 1)])
    return above, below


def taper_of(listed):
    stepped = listed // OWN_BLOCKS
    moved = jnp.abs(stepped // 3 - 1) + jnp.abs(stepped % 3 - 1)
    return jnp.where(moved == 0, 1.0, jnp.where(moved == 1, 0.6, 0.35)).astype(jnp.float32)


def weights_for(candidates, pairs, listed):
    members = candidates.shape[0]
    candidate_count = candidates.shape[1]
    choose_iota = lax.broadcasted_iota(jnp.int32, (LISTED, candidate_count), 1)
    selector = listed[:, None] == choose_iota
    chosen = jnp.concatenate(
        [
            lax.dynamic_slice_in_dim(candidates, listed[j], 1, axis=1).reshape(members, SLOTS)
            for j in range(LISTED)
        ],
        axis=1,
    )
    picked = jnp.einsum(
        "ajs,lj->als", pairs, selector.astype(jnp.float32), precision=exact_precision
    )
    tapering = taper_of(listed)
    widened = barrier(chosen).astype(jnp.float32)
    centre = jnp.mean(widened, axis=0)
    obs_pert = (widened - centre).astype(jnp.bfloat16)
    weight = (picked[1] * tapering[:, None]).reshape(LISTED * SLOTS)
    innovation = picked[0].reshape(LISTED * SLOTS) - centre
    pert_wide = barrier(obs_pert).astype(jnp.float32)
    scaled = (pert_wide * jnp.sqrt(weight)).astype(jnp.bfloat16)
    identity = jnp.eye(members, dtype=jnp.float32)
    system = lax.dot_general(
        scaled, scaled, (((1,), (1,)), ((), ())), preferred_element_type=jnp.float32
    )
    system = system + (members - 1) / 1.1 * identity
    scaling = jnp.sqrt(jnp.sum(system * system))
    iterate = system / scaling
    inverse_root = identity
    for iteration in range(SWEEPS):
        middle = 1.5 * identity - 0.5 * jnp.dot(inverse_root, iterate, precision=exact_precision)
        iterate = jnp.dot(iterate, middle, precision=exact_precision)
        inverse_root = jnp.dot(middle, inverse_root, precision=exact_precision)
    forcing = jnp.dot(pert_wide, weight * innovation, precision=exact_precision)
    inner = jnp.dot(inverse_root, forcing, precision=exact_precision)
    mean_weight = jnp.dot(inverse_root, inner, precision=exact_precision) / scaling
    weights = jnp.sqrt((members - 1) / scaling) * inverse_root + mean_weight[:, None]
    return weights.astype(jnp.bfloat16).T


def apply_kernel(weights_ref, fields_ref, out_ref):
    sources, _, own, columns = fields_ref.shape
    members = sources * own
    wide = fields_ref[...].reshape(sources, own, columns).astype(jnp.float32).reshape(members, columns)
    mean = jnp.sum(wide, axis=0, keepdims=True) * (1.0 / members)
    pert = (wide - mean).astype(jnp.bfloat16)
    updated = jnp.dot(weights_ref[...], pert, preferred_element_type=jnp.float32) + mean
    out_ref[...] = updated.reshape(sources, 1, own, columns).astype(out_ref.dtype)


def apply_weights(weights, fields):
    sources, levels, own, columns = fields.shape
    members = sources * own
    block = pl.BlockSpec((sources, 1, own, columns), lambda v: (0, v, 0, 0))
    return pl.pallas_call(
        apply_kernel,
        grid=(levels,),
        in_specs=[pl.BlockSpec((members, members), lambda v: (0, 0)), block],
        out_specs=block,
        out_shape=jax.ShapeDtypeStruct(fields.shape, fields.dtype),
        compiler_params=pltpu.CompilerParams(vmem_limit_bytes=24 * 1024 * 1024),
        cost_estimate=pl.CostEstimate(
            flops=2 * members * members * levels * columns,
            bytes_accessed=4 * members * levels * columns,
            transcendentals=0,
        ),
    )(weights, fields)


def observe(shaped_fields, where_flat, kernel):
    patch_count = where_flat.shape[0]
    slot_count = where_flat.shape[1]
    column_of = where_flat % COLUMNS
    variable_of = where_flat // COLUMNS
    column_iota = lax.broadcasted_iota(jnp.int32, (patch_count, COLUMNS, slot_count), 1)
    column_hot = (column_of[:, None, :] == column_iota).astype(jnp.bfloat16)
    spread = jnp.einsum(
        "kpvq,pqo->kpvo", shaped_fields, column_hot, preferred_element_type=jnp.float32
    )
    variable_iota = lax.broadcasted_iota(jnp.int32, (patch_count, VARIABLES, slot_count), 1)
    variable_weight = jnp.where(
        variable_of[:, None, :] == variable_iota, kernel[None, :, None], 0.0
    )
    return jnp.sum(spread * variable_weight[None], axis=2)


def body(ensemble, observations, precision, valid_count, position, level_kernel, listed_blocks):
    kernel = level_kernel[0]
    own = ensemble.shape[0]
    row_patches = ensemble.shape[2]
    members = own * row_patches
    fields = ensemble.reshape(own, row_patches, VARIABLES, COLUMNS)

    slot_index = lax.broadcasted_iota(jnp.int32, precision.shape, 3)
    precision_used = jnp.where(slot_index < valid_count[..., None], precision, 0.0)
    table = jnp.concatenate(
        [
            position.reshape(OWN_BLOCKS, SLOTS).astype(jnp.float32),
            observations.reshape(OWN_BLOCKS, SLOTS),
            precision_used.reshape(OWN_BLOCKS, SLOTS),
        ]
    )
    tables = exchange(jnp.broadcast_to(table[None], (row_patches,) + table.shape))

    def outgoing(low, high):
        return fields[:, :, low:high].transpose(1, 2, 0, 3)

    first = outgoing(0, FIRST)
    first, tables = barrier((first, tables))
    first = exchange(first)

    where = tables[:, :OWN_BLOCKS].reshape(row_patches, OWN_BLOCKS * SLOTS).astype(jnp.int32)
    level_term = observe(fields, where, kernel)
    equivalent = lax.psum(level_term, "level").astype(jnp.bfloat16)
    padded = jnp.pad(equivalent, ((0, 0), (1, 1), (0, 0)))
    spread = jnp.concatenate(
        [padded[:, shift : shift + row_patches] for shift in range(3)], axis=2
    ).transpose(1, 0, 2)
    spread, first = barrier((spread, first))
    near = exchange(spread).reshape(members, 3 * OWN_BLOCKS * SLOTS)

    rest = outgoing(FIRST, VARIABLES)
    rest, near = barrier((rest, near))
    rest = exchange(rest)

    here = lax.axis_index("member")
    pair_rows = jnp.pad(tables[:, OWN_BLOCKS:], ((1, 1), (0, 0), (0, 0)))
    pair_own = lax.dynamic_slice_in_dim(pair_rows, here, 3, axis=0)
    pair_above, pair_below = row_halo(pair_own)
    near_above, near_below = row_halo(near)
    candidates = jnp.concatenate([near_above, near, near_below], axis=1)
    candidates = candidates.reshape(members, 9 * OWN_BLOCKS, SLOTS)
    pairs = jnp.concatenate([pair_above, pair_own, pair_below], axis=0)
    pairs = pairs.reshape(9, 2, OWN_BLOCKS, SLOTS).transpose(1, 0, 2, 3)
    pairs = pairs.reshape(2, 9 * OWN_BLOCKS, SLOTS)
    weights = weights_for(candidates, pairs, listed_blocks[0, 0])

    first_out = apply_weights(weights, first)
    first_out, rest = barrier((first_out, rest))
    first_back = exchange(first_out)
    rest_out = apply_weights(weights, rest)
    rest_out, first_back = barrier((rest_out, first_back))
    rest_back = exchange(rest_out)
    result = jnp.concatenate([first_back, rest_back], axis=1)
    result = result.transpose(2, 0, 1, 3)
    return result.reshape(ensemble.shape)


def solution(mesh):
    placed = (
        P("member", "patch", None, "level", None, None),
        P("patch", "member", None, None),
        P("patch", "member", None, None),
        P("patch", "member", None),
        P("patch", "member", None, None),
        P("level", None),
        P("patch", "member", None),
    )
    return jax.shard_map(
        body,
        mesh=mesh,
        in_specs=placed,
        out_specs=P("member", "patch", None, "level", None, None),
        check_vma=False,
    )
```

```python
import jax
import jax.numpy as jnp
from jax import lax
from jax.experimental import pallas as pl
from jax.experimental.pallas import tpu as pltpu
from jax.sharding import PartitionSpec as P

VARIABLES = 12
COLUMNS = 1024
SLOTS = 128
OWN_BLOCKS = 2
LISTED = 8
SWEEPS = 6
FIRST = 4
STEP = 4
DEPTHS = 8
TURNS = 4

exact_precision = lax.Precision.HIGHEST
barrier = lax.optimization_barrier


def exchange(cells):
    return lax.all_to_all(cells, "member", split_axis=0, concat_axis=0, tiled=True)


def row_halo(cells):
    count = lax.axis_size("patch")
    above = lax.ppermute(cells, "patch", [(i, i + 1) for i in range(count - 1)])
    below = lax.ppermute(cells, "patch", [(i + 1, i) for i in range(count - 1)])
    return above, below


def shifted(cells, turn, depth):
    pairs = []
    for y in range(TURNS):
        for z in range(DEPTHS):
            pairs.append((y * DEPTHS + z, (y + turn) % TURNS * DEPTHS + (z + depth) % DEPTHS))
    return lax.ppermute(cells, "member", pairs)


def swapped(cells):
    return lax.ppermute(cells, "level", [(0, 1), (1, 0)])


def cost(values, flops=0):
    return pl.CostEstimate(flops=flops, bytes_accessed=4 * values, transcendentals=0)


WEIGHTS_COST = pl.CostEstimate(flops=0, bytes_accessed=1024, transcendentals=0)
PARAMS = pltpu.CompilerParams(vmem_limit_bytes=56 * 1024 * 1024)
SMALL = pltpu.CompilerParams(vmem_limit_bytes=32 * 1024 * 1024)


def weights_kernel(listed_ref, place_ref, *refs):
    own_refs, other_refs, pair_refs = refs[:3], refs[3:6], refs[6:9]
    weights_ref, sided_ref, scaled_ref = refs[9:]
    members = own_refs[0].shape[0]
    total = jnp.zeros((members, SLOTS), jnp.float32)
    for j in range(LISTED):
        block = listed_ref[j]
        row = lax.div(block, 3 * OWN_BLOCKS)
        inside = lax.rem(block, 3 * OWN_BLOCKS)
        column = lax.div(inside, OWN_BLOCKS)
        which = lax.rem(inside, OWN_BLOCKS)
        away = jnp.abs(row - 1) + jnp.abs(column - 1)
        taper = jnp.where(away == 0, 1.0, jnp.where(away == 1, 0.6, 0.35)).astype(jnp.float32)
        lanes = pl.ds(pl.multiple_of(column * SLOTS, SLOTS), SLOTS)
        near_refs = zip(own_refs, other_refs)
        wide = [
            jnp.where(
                which == place_ref[2],
                own_ref[:, lanes].astype(jnp.float32),
                other_ref[:, lanes].astype(jnp.float32),
            )
            for own_ref, other_ref in near_refs
        ]
        wide = jnp.where(row == 0, wide[0], jnp.where(row == 1, wide[1], wide[2]))
        pair = [ref[column] for ref in pair_refs]
        pair = jnp.where(row == 0, pair[0], jnp.where(row == 1, pair[1], pair[2]))
        observed = jnp.where(which == 0, pair[0:1], pair[1:2])
        weight = jnp.where(which == 0, pair[2:3], pair[3:4]) * taper
        centre = jnp.sum(wide, axis=0, keepdims=True) * (1.0 / members)
        pert = (wide - centre).astype(jnp.bfloat16).astype(jnp.float32)
        scaled_ref[:, j * SLOTS : (j + 1) * SLOTS] = (pert * jnp.sqrt(weight)).astype(jnp.bfloat16)
        total = total + pert * (weight * (observed - centre))
    forcing = jnp.sum(total, axis=1, keepdims=True)
    scaled = scaled_ref[...]
    system = lax.dot_general(
        scaled, scaled, (((1,), (1,)), ((), ())), preferred_element_type=jnp.float32
    )
    rows = lax.broadcasted_iota(jnp.int32, (members, members), 0)
    columns = lax.broadcasted_iota(jnp.int32, (members, members), 1)
    identity = jnp.where(rows == columns, 1.0, 0.0).astype(jnp.float32)
    system = system + (members - 1) / 1.1 * identity
    scaling = jnp.sqrt(
        jnp.sum(jnp.sum(system * system, axis=1, keepdims=True), axis=0, keepdims=True)
    )
    iterate = system / scaling
    inverse_root = 1.5 * identity - 0.5 * iterate
    iterate = jnp.dot(iterate, inverse_root, precision=exact_precision)
    for iteration in range(1, SWEEPS):
        middle = 1.5 * identity - 0.5 * jnp.dot(inverse_root, iterate, precision=exact_precision)
        if iteration < SWEEPS - 1:
            iterate = jnp.dot(iterate, middle, precision=exact_precision)
        inverse_root = jnp.dot(middle, inverse_root, precision=exact_precision)
    forcing = jnp.broadcast_to(forcing, (members, SLOTS))
    inner = jnp.dot(inverse_root, forcing, precision=exact_precision)
    mean_weight = jnp.dot(inverse_root, inner, precision=exact_precision)[:, :1] / scaling
    weights = jnp.sqrt((members - 1) / scaling) * inverse_root + mean_weight
    weights = weights.T.astype(jnp.bfloat16)
    weights_ref[...] = weights

    own = members // (TURNS * DEPTHS)
    group = rows // own
    source_y = lax.rem(place_ref[0] + TURNS - group // DEPTHS, TURNS)
    source_z = lax.rem(place_ref[1] + DEPTHS - lax.rem(group, DEPTHS), DEPTHS)
    source = (source_y * DEPTHS + source_z) * own + lax.rem(rows, own)
    reorder = jnp.where(source == columns, 1.0, 0.0).astype(jnp.bfloat16)
    sided = lax.dot_general(
        weights, reorder, (((1,), (1,)), ((), ())), preferred_element_type=jnp.float32
    )
    sided_ref[...] = sided.astype(jnp.bfloat16)


def weights_for(listed, place, nears, others, pairs):
    members = nears[0].shape[0]
    vmem = pl.BlockSpec(memory_space=pltpu.VMEM)
    smem = pl.BlockSpec(memory_space=pltpu.SMEM)
    return pl.pallas_call(
        weights_kernel,
        in_specs=[smem, smem] + [vmem] * 9,
        out_specs=[vmem] * 2,
        out_shape=[jax.ShapeDtypeStruct((members, members), jnp.bfloat16)] * 2,
        scratch_shapes=[pltpu.VMEM((members, LISTED * SLOTS), jnp.bfloat16)],
        compiler_params=PARAMS,
        cost_estimate=WEIGHTS_COST,
    )(listed, place, *nears, *others, *pairs)


def turned_block(ref):
    return jnp.swapaxes(ref[...].reshape(ref.shape[0], *ref.shape[2:]).astype(jnp.float32), 0, 1)


def patch_at(place_ref, turn, depth):
    y = lax.rem(place_ref[0] + turn, TURNS)
    z = lax.rem(place_ref[1] + depth, DEPTHS)
    return y * DEPTHS + z


def pack_first_kernel(place_ref, fields_ref, *refs):
    out_refs, scratch = refs[:-1], refs[-1]
    scratch[...] = turned_block(fields_ref)
    for depth in range(DEPTHS):
        for turn in range(TURNS):
            block = scratch[patch_at(place_ref, turn, depth)]
            out_refs[depth][turn, 0] = block.astype(jnp.bfloat16)


def pack_first(place, fields, low, count):
    own, _, patches, columns = fields.shape
    return pl.pallas_call(
        pack_first_kernel,
        grid_spec=pltpu.PrefetchScalarGridSpec(
            num_scalar_prefetch=1,
            grid=(count,),
            in_specs=[pl.BlockSpec((own, 1, patches, columns), lambda v, s: (0, v + low, 0, 0))],
            out_specs=[
                pl.BlockSpec((TURNS, 1, own, columns), lambda v, s: (0, v, 0, 0))
                for _ in range(DEPTHS)
            ],
            scratch_shapes=[pltpu.VMEM((patches, own, columns), jnp.float32)],
        ),
        out_shape=[
            jax.ShapeDtypeStruct((TURNS, count, own, columns), fields.dtype) for _ in range(DEPTHS)
        ],
        compiler_params=PARAMS,
        cost_estimate=cost(own * count * patches * columns),
    )(place, fields)


def turn_kernel(fields_ref, out_ref):
    for level in range(fields_ref.shape[1]):
        out_ref[:, level] = jnp.swapaxes(fields_ref[:, level], 0, 1)


def turned(fields, low=0, params=PARAMS):
    outer, levels, inner, columns = fields.shape
    levels = levels - low
    return pl.pallas_call(
        turn_kernel,
        grid=(levels // STEP,),
        in_specs=[pl.BlockSpec((outer, STEP, inner, columns), lambda v: (0, v + low // STEP, 0, 0))],
        out_specs=pl.BlockSpec((inner, STEP, outer, columns), lambda v: (0, v, 0, 0)),
        out_shape=jax.ShapeDtypeStruct((inner, levels, outer, columns), fields.dtype),
        compiler_params=params,
        cost_estimate=cost(fields.size),
    )(fields)


def analyse(weights, wide):
    mean = jnp.sum(wide, axis=0, keepdims=True) * (1.0 / wide.shape[0])
    pert = (wide - mean).astype(jnp.bfloat16)
    return jnp.dot(weights, pert, preferred_element_type=jnp.float32) + mean


def apply_first_kernel(weights_ref, *refs):
    by_depth, by_turn, out_refs = refs[:8], refs[8:11], refs[11:]
    own, columns = by_depth[0].shape[2:]
    parts = [ref[0, 0].astype(jnp.float32) for ref in by_depth]
    for ref in by_turn:
        parts.append(ref[...].astype(jnp.float32).reshape(DEPTHS * own, columns))
    updated = analyse(weights_ref[...], jnp.concatenate(parts, axis=0))
    updated = updated.reshape(len(out_refs), TURNS * DEPTHS // len(out_refs), 1, own, columns)
    for part, ref in enumerate(out_refs):
        ref[...] = updated[part].astype(jnp.bfloat16)


def apply_first(weights, by_depth, by_turn, parts, levels):
    _, count, own, columns = by_depth[0].shape
    members = weights.shape[0]
    groups = TURNS * DEPTHS // parts
    taken = pl.BlockSpec((DEPTHS, 1, own, columns), lambda v: (0, v, 0, 0))
    given = pl.BlockSpec((groups, 1, own, columns), lambda v: (0, v, 0, 0))
    return pl.pallas_call(
        apply_first_kernel,
        grid=(count,),
        in_specs=[pl.BlockSpec((members, members), lambda v: (0, 0))]
        + [pl.BlockSpec((1, 1, own, columns), lambda v: (0, v, 0, 0))] * DEPTHS
        + [taken] * (TURNS - 1),
        out_specs=[given] * parts,
        out_shape=[jax.ShapeDtypeStruct((groups, levels, own, columns), jnp.bfloat16)] * parts,
        compiler_params=PARAMS,
        cost_estimate=cost(members * count * columns, 2 * members * members * count * columns),
    )(weights, *by_depth, *by_turn)


def apply_rest_kernel(weights_ref, fields_ref, _, out_ref):
    sources, levels, own, columns = fields_ref.shape
    for level in range(levels):
        wide = fields_ref[:, level].astype(jnp.float32).reshape(sources * own, columns)
        updated = analyse(weights_ref[...], wide).reshape(sources, own, columns)
        out_ref[:, level] = updated.astype(out_ref.dtype)


def apply_rest(weights, fields, whole):
    sources, levels, own, columns = fields.shape
    members = weights.shape[0]
    low = whole.shape[1] - levels
    return pl.pallas_call(
        apply_rest_kernel,
        grid=(levels // STEP,),
        in_specs=[
            pl.BlockSpec((members, members), lambda v: (0, 0)),
            pl.BlockSpec((sources, STEP, own, columns), lambda v: (0, v, 0, 0)),
            pl.BlockSpec(memory_space=pl.ANY),
        ],
        out_specs=pl.BlockSpec(
            (sources, STEP, own, columns), lambda v: (0, v + low // STEP, 0, 0)
        ),
        out_shape=jax.ShapeDtypeStruct(whole.shape, whole.dtype),
        input_output_aliases={2: 0},
        compiler_params=PARAMS,
        cost_estimate=cost(fields.size, 2 * members * fields.size),
    )(weights, fields, whole)


def observe(shaped_fields, where_flat, kernel):
    patch_count = where_flat.shape[0]
    slot_count = where_flat.shape[1]
    column_of = where_flat % COLUMNS
    variable_of = where_flat // COLUMNS
    column_iota = lax.broadcasted_iota(jnp.int32, (patch_count, COLUMNS, slot_count), 1)
    column_hot = (column_of[:, None, :] == column_iota).astype(jnp.bfloat16)
    spread = jnp.einsum(
        "kpvq,pqo->kpvo", shaped_fields, column_hot, preferred_element_type=jnp.float32
    )
    variable_iota = lax.broadcasted_iota(jnp.int32, (patch_count, VARIABLES, slot_count), 1)
    variable_weight = jnp.where(
        variable_of[:, None, :] == variable_iota, kernel[None, :, None], 0.0
    )
    return jnp.sum(spread * variable_weight[None], axis=2)


def body(ensemble, observations, precision, valid_count, position, level_kernel, listed_blocks):
    kernel = level_kernel[0]
    own = ensemble.shape[0]
    row_patches = ensemble.shape[2]
    members = own * row_patches
    fields = ensemble.reshape(own, row_patches, VARIABLES, COLUMNS)
    turned_fields = fields.transpose(0, 2, 1, 3)
    here = lax.axis_index("member")
    level = lax.axis_index("level")
    place = jnp.stack([here // DEPTHS, here % DEPTHS, level]).astype(jnp.int32)

    slot_index = lax.broadcasted_iota(jnp.int32, precision.shape, 3)
    precision_used = jnp.where(slot_index < valid_count[..., None], precision, 0.0)
    table = jnp.concatenate(
        [
            position.reshape(OWN_BLOCKS, SLOTS).astype(jnp.float32),
            observations.reshape(OWN_BLOCKS, SLOTS),
            precision_used.reshape(OWN_BLOCKS, SLOTS),
        ]
    )
    tables = exchange(jnp.broadcast_to(table[None], (row_patches,) + table.shape))

    packed = pack_first(place, turned_fields, 0, FIRST)
    by_depth = [packed[0]] + [shifted(packed[depth], 0, depth) for depth in range(1, DEPTHS)]

    where = tables[:, :OWN_BLOCKS].reshape(row_patches, OWN_BLOCKS * SLOTS).astype(jnp.int32)
    level_term = observe(fields, where, kernel)
    equivalent = lax.psum(level_term, "level").astype(jnp.bfloat16)
    equivalent = jnp.where(level == 0, equivalent[:, :, :SLOTS], equivalent[:, :, SLOTS:])
    padded = jnp.pad(equivalent, ((0, 0), (1, 1), (0, 0)))
    spread = jnp.concatenate(
        [padded[:, shift : shift + row_patches] for shift in range(3)], axis=2
    ).transpose(1, 0, 2)
    spread, by_depth[1], by_depth[7], by_depth[2], by_depth[6], by_depth[4] = barrier(
        (spread, by_depth[1], by_depth[7], by_depth[2], by_depth[6], by_depth[4])
    )
    near = exchange(spread).reshape(members, 3 * SLOTS)

    outgoing = turned(turned_fields, FIRST)
    outgoing, near, by_depth[3], by_depth[5] = barrier(
        (outgoing, near, by_depth[3], by_depth[5])
    )
    incoming = exchange(outgoing)
    by_turn = [
        shifted(jnp.stack([piece[turn] for piece in by_depth]), turn, 0)
        for turn in range(1, TURNS)
    ]

    pair_rows = jnp.pad(tables[:, OWN_BLOCKS:], ((1, 1), (0, 0), (0, 0)))
    pair_own = lax.dynamic_slice_in_dim(pair_rows, here, 3, axis=0)
    pair_above, pair_below = row_halo(pair_own)
    near_above, near_below = row_halo(near)
    nears = [near_above, near, near_below]
    weights, sided = weights_for(
        listed_blocks[0, 0],
        place,
        nears,
        [swapped(cells) for cells in nears],
        [pair_above, pair_own, pair_below],
    )
    outs = apply_first(sided, by_depth, by_turn, 1, VARIABLES)[0]
    incoming, outs = barrier((incoming, outs))
    outs = apply_rest(weights, incoming, outs)
    whole = turned(exchange(outs), params=SMALL)
    return whole.transpose(0, 2, 1, 3).reshape(ensemble.shape)


def solution(mesh):
    placed = (
        P("member", "patch", None, "level", None, None),
        P("patch", "member", None, None),
        P("patch", "member", None, None),
        P("patch", "member", None),
        P("patch", "member", None, None),
        P("level", None),
        P("patch", "member", None),
    )
    return jax.shard_map(
        body,
        mesh=mesh,
        in_specs=placed,
        out_specs=P("member", "patch", None, "level", None, None),
        check_vma=False,
    )
```

```python
import jax
import jax.numpy as jnp
from jax import lax
from jax.experimental import pallas as pl
from jax.experimental.pallas import tpu as pltpu
from jax.sharding import PartitionSpec as P

VARIABLES = 12
COLUMNS = 1024
SLOTS = 128
OWN_BLOCKS = 2
LISTED = 8
SWEEPS = 6
FIRST = 4
STEP = 4
PAIR = 2
DEPTHS = 8
TURNS = 4

exact_precision = lax.Precision.HIGHEST
barrier = lax.optimization_barrier


def exchange(cells):
    return lax.all_to_all(cells, "member", split_axis=0, concat_axis=0, tiled=True)


def row_halo(cells):
    count = lax.axis_size("patch")
    above = lax.ppermute(cells, "patch", [(i, i + 1) for i in range(count - 1)])
    below = lax.ppermute(cells, "patch", [(i + 1, i) for i in range(count - 1)])
    return above, below


def shifted(cells, turn, depth):
    pairs = []
    for y in range(TURNS):
        for z in range(DEPTHS):
            pairs.append((y * DEPTHS + z, (y + turn) % TURNS * DEPTHS + (z + depth) % DEPTHS))
    return lax.ppermute(cells, "member", pairs)


def swapped(cells):
    return lax.ppermute(cells, "level", [(0, 1), (1, 0)])


def cost(values, flops=0):
    return pl.CostEstimate(flops=flops, bytes_accessed=4 * values, transcendentals=0)


WEIGHTS_COST = pl.CostEstimate(flops=0, bytes_accessed=1024, transcendentals=0)
PARAMS = pltpu.CompilerParams(vmem_limit_bytes=56 * 1024 * 1024)
SMALL = pltpu.CompilerParams(vmem_limit_bytes=32 * 1024 * 1024)


def weights_kernel(listed_ref, place_ref, *refs):
    own_refs, other_refs, pair_refs = refs[:3], refs[3:6], refs[6:9]
    weights_ref, sided_ref, scaled_ref = refs[9:]
    members = own_refs[0].shape[0]
    total = jnp.zeros((members, SLOTS), jnp.float32)
    for j in range(LISTED):
        block = listed_ref[j]
        row = lax.div(block, 3 * OWN_BLOCKS)
        inside = lax.rem(block, 3 * OWN_BLOCKS)
        column = lax.div(inside, OWN_BLOCKS)
        which = lax.rem(inside, OWN_BLOCKS)
        away = jnp.abs(row - 1) + jnp.abs(column - 1)
        taper = jnp.where(away == 0, 1.0, jnp.where(away == 1, 0.6, 0.35)).astype(jnp.float32)
        lanes = pl.ds(pl.multiple_of(column * SLOTS, SLOTS), SLOTS)
        near_refs = zip(own_refs, other_refs)
        wide = [
            jnp.where(
                which == place_ref[2],
                own_ref[:, lanes].astype(jnp.float32),
                other_ref[:, lanes].astype(jnp.float32),
            )
            for own_ref, other_ref in near_refs
        ]
        wide = jnp.where(row == 0, wide[0], jnp.where(row == 1, wide[1], wide[2]))
        pair = [ref[column] for ref in pair_refs]
        pair = jnp.where(row == 0, pair[0], jnp.where(row == 1, pair[1], pair[2]))
        observed = jnp.where(which == 0, pair[0:1], pair[1:2])
        weight = jnp.where(which == 0, pair[2:3], pair[3:4]) * taper
        centre = jnp.sum(wide, axis=0, keepdims=True) * (1.0 / members)
        pert = (wide - centre).astype(jnp.bfloat16).astype(jnp.float32)
        scaled_ref[:, j * SLOTS : (j + 1) * SLOTS] = (pert * jnp.sqrt(weight)).astype(jnp.bfloat16)
        total = total + pert * (weight * (observed - centre))
    forcing = jnp.sum(total, axis=1, keepdims=True)
    scaled = scaled_ref[...]
    system = lax.dot_general(
        scaled, scaled, (((1,), (1,)), ((), ())), preferred_element_type=jnp.float32
    )
    rows = lax.broadcasted_iota(jnp.int32, (members, members), 0)
    columns = lax.broadcasted_iota(jnp.int32, (members, members), 1)
    identity = jnp.where(rows == columns, 1.0, 0.0).astype(jnp.float32)
    system = system + (members - 1) / 1.1 * identity
    scaling = jnp.sqrt(
        jnp.sum(jnp.sum(system * system, axis=1, keepdims=True), axis=0, keepdims=True)
    )
    iterate = system / scaling
    inverse_root = 1.5 * identity - 0.5 * iterate
    iterate = jnp.dot(iterate, inverse_root, precision=exact_precision)
    for iteration in range(1, SWEEPS):
        middle = 1.5 * identity - 0.5 * jnp.dot(inverse_root, iterate, precision=exact_precision)
        if iteration < SWEEPS - 1:
            iterate = jnp.dot(iterate, middle, precision=exact_precision)
        inverse_root = jnp.dot(middle, inverse_root, precision=exact_precision)
    forcing = jnp.broadcast_to(forcing, (members, SLOTS))
    inner = jnp.dot(inverse_root, forcing, precision=exact_precision)
    mean_weight = jnp.dot(inverse_root, inner, precision=exact_precision)[:, :1] / scaling
    weights = jnp.sqrt((members - 1) / scaling) * inverse_root + mean_weight
    weights = weights.T.astype(jnp.bfloat16)
    weights_ref[...] = weights

    own = members // (TURNS * DEPTHS)
    group = rows // own
    source_y = lax.rem(place_ref[0] + TURNS - group // DEPTHS, TURNS)
    source_z = lax.rem(place_ref[1] + DEPTHS - lax.rem(group, DEPTHS), DEPTHS)
    source = (source_y * DEPTHS + source_z) * own + lax.rem(rows, own)
    reorder = jnp.where(source == columns, 1.0, 0.0).astype(jnp.bfloat16)
    sided = lax.dot_general(
        weights, reorder, (((1,), (1,)), ((), ())), preferred_element_type=jnp.float32
    )
    sided_ref[...] = sided.astype(jnp.bfloat16)


def weights_for(listed, place, nears, others, pairs):
    members = nears[0].shape[0]
    vmem = pl.BlockSpec(memory_space=pltpu.VMEM)
    smem = pl.BlockSpec(memory_space=pltpu.SMEM)
    return pl.pallas_call(
        weights_kernel,
        in_specs=[smem, smem] + [vmem] * 9,
        out_specs=[vmem] * 2,
        out_shape=[jax.ShapeDtypeStruct((members, members), jnp.bfloat16)] * 2,
        scratch_shapes=[pltpu.VMEM((members, LISTED * SLOTS), jnp.bfloat16)],
        compiler_params=PARAMS,
        cost_estimate=WEIGHTS_COST,
    )(listed, place, *nears, *others, *pairs)


def patch_at(place_ref, turn, depth):
    y = lax.rem(place_ref[0] + turn, TURNS)
    z = lax.rem(place_ref[1] + depth, DEPTHS)
    return y * DEPTHS + z


def pack_first_kernel(place_ref, fields_ref, *refs):
    out_refs, scratch = refs[:-1], refs[-1]
    for level in range(PAIR):
        scratch[...] = jnp.swapaxes(fields_ref[:, level], 0, 1)
        for depth in range(DEPTHS):
            for turn in range(TURNS):
                out_refs[depth][turn, level] = scratch[patch_at(place_ref, turn, depth)]


def pack_first(place, fields, count):
    own, _, patches, columns = fields.shape
    return pl.pallas_call(
        pack_first_kernel,
        grid_spec=pltpu.PrefetchScalarGridSpec(
            num_scalar_prefetch=1,
            grid=(count // PAIR,),
            in_specs=[pl.BlockSpec((own, PAIR, patches, columns), lambda v, s: (0, v, 0, 0))],
            out_specs=[
                pl.BlockSpec((TURNS, PAIR, own, columns), lambda v, s: (0, v, 0, 0))
                for _ in range(DEPTHS)
            ],
            scratch_shapes=[pltpu.VMEM((patches, own, columns), fields.dtype)],
        ),
        out_shape=[
            jax.ShapeDtypeStruct((TURNS, count, own, columns), fields.dtype) for _ in range(DEPTHS)
        ],
        compiler_params=PARAMS,
        cost_estimate=cost(own * count * patches * columns),
    )(place, fields)


def table_kernel(count_ref, position_ref, observed_ref, precision_ref, out_ref):
    slot = lax.broadcasted_iota(jnp.int32, (1, SLOTS), 1)
    used = [
        jnp.where(slot < count_ref[block], precision_ref[block : block + 1], 0.0)
        for block in range(OWN_BLOCKS)
    ]
    table = jnp.concatenate(
        [position_ref[...].astype(jnp.float32), observed_ref[...]] + used, axis=0
    )
    out_ref[...] = jnp.broadcast_to(table[None], out_ref.shape)


def table_of(count, position, observed, precision, patches):
    vmem = pl.BlockSpec(memory_space=pltpu.VMEM)
    return pl.pallas_call(
        table_kernel,
        in_specs=[pl.BlockSpec(memory_space=pltpu.SMEM)] + [vmem] * 3,
        out_specs=vmem,
        out_shape=jax.ShapeDtypeStruct((patches, 3 * OWN_BLOCKS, SLOTS), jnp.float32),
    )(count, position, observed, precision)


def turn_kernel(fields_ref, out_ref):
    for level in range(fields_ref.shape[1]):
        out_ref[:, level] = jnp.swapaxes(fields_ref[:, level], 0, 1)


def turned(fields, low=0, params=PARAMS):
    outer, levels, inner, columns = fields.shape
    levels = levels - low
    return pl.pallas_call(
        turn_kernel,
        grid=(levels // STEP,),
        in_specs=[pl.BlockSpec((outer, STEP, inner, columns), lambda v: (0, v + low // STEP, 0, 0))],
        out_specs=pl.BlockSpec((inner, STEP, outer, columns), lambda v: (0, v, 0, 0)),
        out_shape=jax.ShapeDtypeStruct((inner, levels, outer, columns), fields.dtype),
        compiler_params=params,
        cost_estimate=cost(fields.size),
    )(fields)


def gather_kernel(*refs):
    by_depth, by_turn = refs[:DEPTHS], refs[DEPTHS:]
    for turn in range(1, TURNS):
        for depth in range(DEPTHS):
            by_turn[turn - 1][depth] = by_depth[depth][turn]


def gathered(by_depth):
    turns, count, own, columns = by_depth[0].shape
    return pl.pallas_call(
        gather_kernel,
        grid=(count // PAIR,),
        in_specs=[pl.BlockSpec((turns, PAIR, own, columns), lambda v: (0, v, 0, 0))] * DEPTHS,
        out_specs=[pl.BlockSpec((DEPTHS, PAIR, own, columns), lambda v: (0, v, 0, 0))] * (turns - 1),
        out_shape=[
            jax.ShapeDtypeStruct((DEPTHS, count, own, columns), by_depth[0].dtype)
            for _ in range(turns - 1)
        ],
        compiler_params=PARAMS,
        cost_estimate=pl.CostEstimate(flops=0, bytes_accessed=1 << 22, transcendentals=0),
    )(*by_depth)


def passed_kernel(cells_ref, out_ref):
    out_ref[...] = cells_ref[...]


def passed(cells):
    vmem = pl.BlockSpec(memory_space=pltpu.VMEM)
    return pl.pallas_call(
        passed_kernel,
        in_specs=[vmem],
        out_specs=vmem,
        out_shape=jax.ShapeDtypeStruct(cells.shape, cells.dtype),
        compiler_params=PARAMS,
        cost_estimate=pl.CostEstimate(flops=1 << 40, bytes_accessed=1 << 31, transcendentals=0),
    )(cells)


def analyse(weights, wide):
    mean = jnp.sum(wide, axis=0, keepdims=True) * (1.0 / wide.shape[0])
    pert = (wide - mean).astype(jnp.bfloat16)
    return jnp.dot(weights, pert, preferred_element_type=jnp.float32) + mean


def apply_first_kernel(weights_ref, *refs):
    by_depth, by_turn, out_ref = refs[:DEPTHS], refs[DEPTHS:-1], refs[-1]
    own, columns = by_depth[0].shape[2:]
    for level in range(PAIR):
        parts = [ref[0, level].astype(jnp.float32) for ref in by_depth]
        for ref in by_turn:
            parts.append(ref[:, level].astype(jnp.float32).reshape(DEPTHS * own, columns))
        updated = analyse(weights_ref[...], jnp.concatenate(parts, axis=0))
        updated = updated.reshape(TURNS * DEPTHS, own, columns)
        out_ref[:, level] = updated.astype(out_ref.dtype)


def apply_first(weights, by_depth, by_turn, levels):
    _, count, own, columns = by_depth[0].shape
    members = weights.shape[0]
    groups = TURNS * DEPTHS
    return pl.pallas_call(
        apply_first_kernel,
        grid=(count // PAIR,),
        in_specs=[pl.BlockSpec((members, members), lambda v: (0, 0))]
        + [pl.BlockSpec((1, PAIR, own, columns), lambda v: (0, v, 0, 0))] * DEPTHS
        + [pl.BlockSpec((DEPTHS, PAIR, own, columns), lambda v: (0, v, 0, 0))] * (TURNS - 1),
        out_specs=pl.BlockSpec((groups, PAIR, own, columns), lambda v: (0, v, 0, 0)),
        out_shape=jax.ShapeDtypeStruct((groups, levels, own, columns), jnp.bfloat16),
        compiler_params=PARAMS,
        cost_estimate=cost(members * count * columns, 2 * members * members * count * columns),
    )(weights, *by_depth, *by_turn)


def apply_rest_kernel(weights_ref, fields_ref, _, out_ref):
    sources, levels, own, columns = fields_ref.shape
    for level in range(levels):
        wide = fields_ref[:, level].astype(jnp.float32).reshape(sources * own, columns)
        updated = analyse(weights_ref[...], wide).reshape(sources, own, columns)
        out_ref[:, level] = updated.astype(out_ref.dtype)


def apply_rest(weights, fields, whole):
    sources, levels, own, columns = fields.shape
    members = weights.shape[0]
    low = whole.shape[1] - levels
    return pl.pallas_call(
        apply_rest_kernel,
        grid=(levels // STEP,),
        in_specs=[
            pl.BlockSpec((members, members), lambda v: (0, 0)),
            pl.BlockSpec((sources, STEP, own, columns), lambda v: (0, v, 0, 0)),
            pl.BlockSpec(memory_space=pl.ANY),
        ],
        out_specs=pl.BlockSpec(
            (sources, STEP, own, columns), lambda v: (0, v + low // STEP, 0, 0)
        ),
        out_shape=jax.ShapeDtypeStruct(whole.shape, whole.dtype),
        input_output_aliases={2: 0},
        compiler_params=PARAMS,
        cost_estimate=cost(fields.size, 2 * members * fields.size),
    )(weights, fields, whole)


def observe(shaped_fields, where_flat, kernel):
    patch_count = where_flat.shape[0]
    slot_count = where_flat.shape[1]
    column_of = where_flat % COLUMNS
    variable_of = where_flat // COLUMNS
    column_iota = lax.broadcasted_iota(jnp.int32, (patch_count, COLUMNS, slot_count), 1)
    column_hot = (column_of[:, None, :] == column_iota).astype(jnp.bfloat16)
    spread = jnp.einsum(
        "kpvq,pqo->kpvo", shaped_fields, column_hot, preferred_element_type=jnp.float32
    )
    variable_iota = lax.broadcasted_iota(jnp.int32, (patch_count, VARIABLES, slot_count), 1)
    variable_weight = jnp.where(
        variable_of[:, None, :] == variable_iota, kernel[None, :, None], 0.0
    )
    return jnp.sum(spread * variable_weight[None], axis=2)


def body(ensemble, observations, precision, valid_count, position, level_kernel, listed_blocks):
    kernel = level_kernel[0]
    own = ensemble.shape[0]
    row_patches = ensemble.shape[2]
    members = own * row_patches
    fields = ensemble.reshape(own, row_patches, VARIABLES, COLUMNS)
    turned_fields = fields.transpose(0, 2, 1, 3)
    here = lax.axis_index("member")
    level = lax.axis_index("level")
    place = jnp.stack([here // DEPTHS, here % DEPTHS, level]).astype(jnp.int32)

    tables = exchange(
        table_of(
            valid_count.reshape(OWN_BLOCKS),
            position.reshape(OWN_BLOCKS, SLOTS),
            observations.reshape(OWN_BLOCKS, SLOTS),
            precision.reshape(OWN_BLOCKS, SLOTS),
            row_patches,
        )
    )

    packed = pack_first(place, turned_fields, FIRST)
    by_depth = [packed[0]] + [shifted(packed[depth], 0, depth) for depth in range(1, DEPTHS)]

    where = tables[:, :OWN_BLOCKS].reshape(row_patches, OWN_BLOCKS * SLOTS).astype(jnp.int32)
    level_term = observe(fields, where, kernel)
    equivalent = lax.psum(level_term, "level").astype(jnp.bfloat16)
    equivalent = jnp.where(level == 0, equivalent[:, :, :SLOTS], equivalent[:, :, SLOTS:])
    padded = jnp.pad(equivalent, ((0, 0), (1, 1), (0, 0)))
    spread = jnp.concatenate(
        [padded[:, shift : shift + row_patches] for shift in range(3)], axis=2
    ).transpose(1, 0, 2)
    spread, by_depth[1], by_depth[7], by_depth[2], by_depth[6], by_depth[4] = barrier(
        (spread, by_depth[1], by_depth[7], by_depth[2], by_depth[6], by_depth[4])
    )
    near = exchange(spread).reshape(members, 3 * SLOTS)

    outgoing = turned(turned_fields, FIRST)
    outgoing, near = barrier((outgoing, near))
    near = passed(near)
    near, by_depth[3], by_depth[5] = barrier((near, by_depth[3], by_depth[5]))
    incoming = exchange(outgoing)
    by_turn = gathered(by_depth)
    by_turn = [shifted(by_turn[turn - 1], turn, 0) for turn in range(1, TURNS)]

    pair_rows = jnp.pad(tables[:, OWN_BLOCKS:], ((1, 1), (0, 0), (0, 0)))
    pair_own = lax.dynamic_slice_in_dim(pair_rows, here, 3, axis=0)
    pair_above, pair_below = row_halo(pair_own)
    near_above, near_below = row_halo(near)
    nears = [near_above, near, near_below]
    weights, sided = weights_for(
        listed_blocks[0, 0],
        place,
        nears,
        [swapped(cells) for cells in nears],
        [pair_above, pair_own, pair_below],
    )
    outs = apply_first(sided, by_depth, by_turn, VARIABLES)
    incoming, outs = barrier((incoming, outs))
    outs = apply_rest(weights, incoming, outs)
    whole = turned(exchange(outs), params=SMALL)
    return whole.transpose(0, 2, 1, 3).reshape(ensemble.shape)


def solution(mesh):
    placed = (
        P("member", "patch", None, "level", None, None),
        P("patch", "member", None, None),
        P("patch", "member", None, None),
        P("patch", "member", None),
        P("patch", "member", None, None),
        P("level", None),
        P("patch", "member", None),
    )
    return jax.shard_map(
        body,
        mesh=mesh,
        in_specs=placed,
        out_specs=P("member", "patch", None, "level", None, None),
        check_vma=False,
    )
```

```python
import jax
import jax.numpy as jnp
from jax import lax
from jax.experimental import pallas as pl
from jax.experimental.pallas import tpu as pltpu
from jax.sharding import PartitionSpec as P

VARIABLES = 12
COLUMNS = 1024
SLOTS = 128
OWN_BLOCKS = 2
LISTED = 8
SWEEPS = 6
FIRST = 6
STEP = 3
PAIR = 2
DEPTHS = 8
TURNS = 4

exact_precision = lax.Precision.HIGHEST
barrier = lax.optimization_barrier


def exchange(cells):
    return lax.all_to_all(cells, "member", split_axis=0, concat_axis=0, tiled=True)


def row_halo(cells):
    count = lax.axis_size("patch")
    above = lax.ppermute(cells, "patch", [(i, i + 1) for i in range(count - 1)])
    below = lax.ppermute(cells, "patch", [(i + 1, i) for i in range(count - 1)])
    return above, below


def shifted(cells, turn, depth):
    pairs = []
    for y in range(TURNS):
        for z in range(DEPTHS):
            pairs.append((y * DEPTHS + z, (y + turn) % TURNS * DEPTHS + (z + depth) % DEPTHS))
    return lax.ppermute(cells, "member", pairs)


def swapped(cells):
    return lax.ppermute(cells, "level", [(0, 1), (1, 0)])


def cost(values, flops=0):
    return pl.CostEstimate(flops=flops, bytes_accessed=4 * values, transcendentals=0)


WEIGHTS_COST = pl.CostEstimate(flops=0, bytes_accessed=1024, transcendentals=0)
PARAMS = pltpu.CompilerParams(vmem_limit_bytes=56 * 1024 * 1024)
SMALL = pltpu.CompilerParams(vmem_limit_bytes=32 * 1024 * 1024)


def weights_kernel(listed_ref, place_ref, *refs):
    own_refs, other_refs, pair_refs = refs[:3], refs[3:6], refs[6:9]
    weights_ref, sided_ref, scaled_ref = refs[9:]
    members = own_refs[0].shape[0]
    total = jnp.zeros((members, SLOTS), jnp.float32)
    for j in range(LISTED):
        block = listed_ref[j]
        row = lax.div(block, 3 * OWN_BLOCKS)
        inside = lax.rem(block, 3 * OWN_BLOCKS)
        column = lax.div(inside, OWN_BLOCKS)
        which = lax.rem(inside, OWN_BLOCKS)
        away = jnp.abs(row - 1) + jnp.abs(column - 1)
        taper = jnp.where(away == 0, 1.0, jnp.where(away == 1, 0.6, 0.35)).astype(jnp.float32)
        lanes = pl.ds(pl.multiple_of(column * SLOTS, SLOTS), SLOTS)
        near_refs = zip(own_refs, other_refs)
        wide = [
            jnp.where(
                which == place_ref[2],
                own_ref[:, lanes].astype(jnp.float32),
                other_ref[:, lanes].astype(jnp.float32),
            )
            for own_ref, other_ref in near_refs
        ]
        wide = jnp.where(row == 0, wide[0], jnp.where(row == 1, wide[1], wide[2]))
        pair = [ref[column] for ref in pair_refs]
        pair = jnp.where(row == 0, pair[0], jnp.where(row == 1, pair[1], pair[2]))
        observed = jnp.where(which == 0, pair[0:1], pair[1:2])
        weight = jnp.where(which == 0, pair[2:3], pair[3:4]) * taper
        centre = jnp.sum(wide, axis=0, keepdims=True) * (1.0 / members)
        pert = (wide - centre).astype(jnp.bfloat16).astype(jnp.float32)
        scaled_ref[:, j * SLOTS : (j + 1) * SLOTS] = (pert * jnp.sqrt(weight)).astype(jnp.bfloat16)
        total = total + pert * (weight * (observed - centre))
    forcing = jnp.sum(total, axis=1, keepdims=True)
    scaled = scaled_ref[...]
    system = lax.dot_general(
        scaled, scaled, (((1,), (1,)), ((), ())), preferred_element_type=jnp.float32
    )
    rows = lax.broadcasted_iota(jnp.int32, (members, members), 0)
    columns = lax.broadcasted_iota(jnp.int32, (members, members), 1)
    identity = jnp.where(rows == columns, 1.0, 0.0).astype(jnp.float32)
    system = system + (members - 1) / 1.1 * identity
    scaling = jnp.sqrt(
        jnp.sum(jnp.sum(system * system, axis=1, keepdims=True), axis=0, keepdims=True)
    )
    iterate = system / scaling
    inverse_root = 1.5 * identity - 0.5 * iterate
    iterate = jnp.dot(iterate, inverse_root, precision=exact_precision)
    for iteration in range(1, SWEEPS):
        middle = 1.5 * identity - 0.5 * jnp.dot(inverse_root, iterate, precision=exact_precision)
        if iteration < SWEEPS - 1:
            iterate = jnp.dot(iterate, middle, precision=exact_precision)
        inverse_root = jnp.dot(middle, inverse_root, precision=exact_precision)
    forcing = jnp.broadcast_to(forcing, (members, SLOTS))
    inner = jnp.dot(inverse_root, forcing, precision=exact_precision)
    mean_weight = jnp.dot(inverse_root, inner, precision=exact_precision)[:, :1] / scaling
    weights = jnp.sqrt((members - 1) / scaling) * inverse_root + mean_weight
    weights = weights.T.astype(jnp.bfloat16)
    weights_ref[...] = weights

    own = members // (TURNS * DEPTHS)
    group = rows // own
    source_y = lax.rem(place_ref[0] + TURNS - group // DEPTHS, TURNS)
    source_z = lax.rem(place_ref[1] + DEPTHS - lax.rem(group, DEPTHS), DEPTHS)
    source = (source_y * DEPTHS + source_z) * own + lax.rem(rows, own)
    reorder = jnp.where(source == columns, 1.0, 0.0).astype(jnp.bfloat16)
    sided = lax.dot_general(
        weights, reorder, (((1,), (1,)), ((), ())), preferred_element_type=jnp.float32
    )
    sided_ref[...] = sided.astype(jnp.bfloat16)


def weights_for(listed, place, nears, others, pairs):
    members = nears[0].shape[0]
    vmem = pl.BlockSpec(memory_space=pltpu.VMEM)
    smem = pl.BlockSpec(memory_space=pltpu.SMEM)
    return pl.pallas_call(
        weights_kernel,
        in_specs=[smem, smem] + [vmem] * 9,
        out_specs=[vmem] * 2,
        out_shape=[jax.ShapeDtypeStruct((members, members), jnp.bfloat16)] * 2,
        scratch_shapes=[pltpu.VMEM((members, LISTED * SLOTS), jnp.bfloat16)],
        compiler_params=PARAMS,
        cost_estimate=WEIGHTS_COST,
    )(listed, place, *nears, *others, *pairs)


def patch_at(place_ref, turn, depth):
    y = lax.rem(place_ref[0] + turn, TURNS)
    z = lax.rem(place_ref[1] + depth, DEPTHS)
    return y * DEPTHS + z


def pack_first_kernel(place_ref, fields_ref, *refs):
    out_refs, scratch = refs[:-1], refs[-1]
    for level in range(PAIR):
        scratch[...] = jnp.swapaxes(fields_ref[:, level], 0, 1)
        for depth in range(DEPTHS):
            for turn in range(TURNS):
                out_refs[depth][turn, level] = scratch[patch_at(place_ref, turn, depth)]


def pack_first(place, fields, count):
    own, _, patches, columns = fields.shape
    return pl.pallas_call(
        pack_first_kernel,
        grid_spec=pltpu.PrefetchScalarGridSpec(
            num_scalar_prefetch=1,
            grid=(count // PAIR,),
            in_specs=[pl.BlockSpec((own, PAIR, patches, columns), lambda v, s: (0, v, 0, 0))],
            out_specs=[
                pl.BlockSpec((TURNS, PAIR, own, columns), lambda v, s: (0, v, 0, 0))
                for _ in range(DEPTHS)
            ],
            scratch_shapes=[pltpu.VMEM((patches, own, columns), fields.dtype)],
        ),
        out_shape=[
            jax.ShapeDtypeStruct((TURNS, count, own, columns), fields.dtype) for _ in range(DEPTHS)
        ],
        compiler_params=PARAMS,
        cost_estimate=cost(own * count * patches * columns),
    )(place, fields)


def table_kernel(count_ref, position_ref, observed_ref, precision_ref, out_ref):
    slot = lax.broadcasted_iota(jnp.int32, (1, SLOTS), 1)
    used = [
        jnp.where(slot < count_ref[block], precision_ref[block : block + 1], 0.0)
        for block in range(OWN_BLOCKS)
    ]
    table = jnp.concatenate(
        [position_ref[...].astype(jnp.float32), observed_ref[...]] + used, axis=0
    )
    out_ref[...] = jnp.broadcast_to(table[None], out_ref.shape)


def table_of(count, position, observed, precision, patches):
    vmem = pl.BlockSpec(memory_space=pltpu.VMEM)
    return pl.pallas_call(
        table_kernel,
        in_specs=[pl.BlockSpec(memory_space=pltpu.SMEM)] + [vmem] * 3,
        out_specs=vmem,
        out_shape=jax.ShapeDtypeStruct((patches, 3 * OWN_BLOCKS, SLOTS), jnp.float32),
    )(count, position, observed, precision)


def turn_kernel(fields_ref, out_ref):
    for level in range(fields_ref.shape[1]):
        out_ref[:, level] = jnp.swapaxes(fields_ref[:, level], 0, 1)


def turned(fields, low=0, params=PARAMS):
    outer, levels, inner, columns = fields.shape
    levels = levels - low
    return pl.pallas_call(
        turn_kernel,
        grid=(levels // STEP,),
        in_specs=[pl.BlockSpec((outer, STEP, inner, columns), lambda v: (0, v + low // STEP, 0, 0))],
        out_specs=pl.BlockSpec((inner, STEP, outer, columns), lambda v: (0, v, 0, 0)),
        out_shape=jax.ShapeDtypeStruct((inner, levels, outer, columns), fields.dtype),
        compiler_params=params,
        cost_estimate=cost(fields.size),
    )(fields)


def gather_kernel(*refs):
    by_depth, by_turn = refs[:DEPTHS], refs[DEPTHS:]
    for turn in range(1, TURNS):
        for depth in range(DEPTHS):
            by_turn[turn - 1][depth] = by_depth[depth][turn]


def gathered(by_depth):
    turns, count, own, columns = by_depth[0].shape
    return pl.pallas_call(
        gather_kernel,
        grid=(count // PAIR,),
        in_specs=[pl.BlockSpec((turns, PAIR, own, columns), lambda v: (0, v, 0, 0))] * DEPTHS,
        out_specs=[pl.BlockSpec((DEPTHS, PAIR, own, columns), lambda v: (0, v, 0, 0))] * (turns - 1),
        out_shape=[
            jax.ShapeDtypeStruct((DEPTHS, count, own, columns), by_depth[0].dtype)
            for _ in range(turns - 1)
        ],
        compiler_params=PARAMS,
        cost_estimate=pl.CostEstimate(flops=0, bytes_accessed=1 << 22, transcendentals=0),
    )(*by_depth)


def passed_kernel(cells_ref, out_ref):
    out_ref[...] = cells_ref[...]


def passed(cells):
    vmem = pl.BlockSpec(memory_space=pltpu.VMEM)
    return pl.pallas_call(
        passed_kernel,
        in_specs=[vmem],
        out_specs=vmem,
        out_shape=jax.ShapeDtypeStruct(cells.shape, cells.dtype),
        compiler_params=PARAMS,
        cost_estimate=pl.CostEstimate(flops=1 << 40, bytes_accessed=1 << 31, transcendentals=0),
    )(cells)


def analyse(weights, wide):
    mean = jnp.sum(wide, axis=0, keepdims=True) * (1.0 / wide.shape[0])
    pert = (wide - mean).astype(jnp.bfloat16)
    return jnp.dot(weights, pert, preferred_element_type=jnp.float32) + mean


def apply_first_kernel(weights_ref, *refs):
    by_depth, by_turn, out_ref = refs[:DEPTHS], refs[DEPTHS:-1], refs[-1]
    own, columns = by_depth[0].shape[2:]
    for level in range(PAIR):
        parts = [ref[0, level].astype(jnp.float32) for ref in by_depth]
        for ref in by_turn:
            parts.append(ref[:, level].astype(jnp.float32).reshape(DEPTHS * own, columns))
        updated = analyse(weights_ref[...], jnp.concatenate(parts, axis=0))
        updated = updated.reshape(TURNS * DEPTHS, own, columns)
        out_ref[:, level] = updated.astype(out_ref.dtype)


def apply_first(weights, by_depth, by_turn, levels):
    _, count, own, columns = by_depth[0].shape
    members = weights.shape[0]
    groups = TURNS * DEPTHS
    return pl.pallas_call(
        apply_first_kernel,
        grid=(count // PAIR,),
        in_specs=[pl.BlockSpec((members, members), lambda v: (0, 0))]
        + [pl.BlockSpec((1, PAIR, own, columns), lambda v: (0, v, 0, 0))] * DEPTHS
        + [pl.BlockSpec((DEPTHS, PAIR, own, columns), lambda v: (0, v, 0, 0))] * (TURNS - 1),
        out_specs=pl.BlockSpec((groups, PAIR, own, columns), lambda v: (0, v, 0, 0)),
        out_shape=jax.ShapeDtypeStruct((groups, levels, own, columns), jnp.bfloat16),
        compiler_params=PARAMS,
        cost_estimate=cost(members * count * columns, 2 * members * members * count * columns),
    )(weights, *by_depth, *by_turn)


def apply_rest_kernel(weights_ref, fields_ref, _, out_ref):
    sources, levels, own, columns = fields_ref.shape
    for level in range(levels):
        wide = fields_ref[:, level].astype(jnp.float32).reshape(sources * own, columns)
        updated = analyse(weights_ref[...], wide).reshape(sources, own, columns)
        out_ref[:, level] = updated.astype(out_ref.dtype)


def apply_rest(weights, fields, whole):
    sources, levels, own, columns = fields.shape
    members = weights.shape[0]
    low = whole.shape[1] - levels
    return pl.pallas_call(
        apply_rest_kernel,
        grid=(levels // STEP,),
        in_specs=[
            pl.BlockSpec((members, members), lambda v: (0, 0)),
            pl.BlockSpec((sources, STEP, own, columns), lambda v: (0, v, 0, 0)),
            pl.BlockSpec(memory_space=pl.ANY),
        ],
        out_specs=pl.BlockSpec(
            (sources, STEP, own, columns), lambda v: (0, v + low // STEP, 0, 0)
        ),
        out_shape=jax.ShapeDtypeStruct(whole.shape, whole.dtype),
        input_output_aliases={2: 0},
        compiler_params=PARAMS,
        cost_estimate=cost(fields.size, 2 * members * fields.size),
    )(weights, fields, whole)


def observe(shaped_fields, where_flat, kernel):
    patch_count = where_flat.shape[0]
    slot_count = where_flat.shape[1]
    column_of = where_flat % COLUMNS
    variable_of = where_flat // COLUMNS
    column_iota = lax.broadcasted_iota(jnp.int32, (patch_count, COLUMNS, slot_count), 1)
    column_hot = (column_of[:, None, :] == column_iota).astype(jnp.bfloat16)
    spread = jnp.einsum(
        "kpvq,pqo->kpvo", shaped_fields, column_hot, preferred_element_type=jnp.float32
    )
    variable_iota = lax.broadcasted_iota(jnp.int32, (patch_count, VARIABLES, slot_count), 1)
    variable_weight = jnp.where(
        variable_of[:, None, :] == variable_iota, kernel[None, :, None], 0.0
    )
    return jnp.sum(spread * variable_weight[None], axis=2)


def body(ensemble, observations, precision, valid_count, position, level_kernel, listed_blocks):
    kernel = level_kernel[0]
    own = ensemble.shape[0]
    row_patches = ensemble.shape[2]
    members = own * row_patches
    fields = ensemble.reshape(own, row_patches, VARIABLES, COLUMNS)
    turned_fields = fields.transpose(0, 2, 1, 3)
    here = lax.axis_index("member")
    level = lax.axis_index("level")
    place = jnp.stack([here // DEPTHS, here % DEPTHS, level]).astype(jnp.int32)

    tables = exchange(
        table_of(
            valid_count.reshape(OWN_BLOCKS),
            position.reshape(OWN_BLOCKS, SLOTS),
            observations.reshape(OWN_BLOCKS, SLOTS),
            precision.reshape(OWN_BLOCKS, SLOTS),
            row_patches,
        )
    )

    packed = pack_first(place, turned_fields, FIRST)
    by_depth = [packed[0]] + [shifted(packed[depth], 0, depth) for depth in range(1, DEPTHS)]

    where = tables[:, :OWN_BLOCKS].reshape(row_patches, OWN_BLOCKS * SLOTS).astype(jnp.int32)
    level_term = observe(fields, where, kernel)
    equivalent = lax.psum(level_term, "level").astype(jnp.bfloat16)
    equivalent = jnp.where(level == 0, equivalent[:, :, :SLOTS], equivalent[:, :, SLOTS:])
    padded = jnp.pad(equivalent, ((0, 0), (1, 1), (0, 0)))
    spread = jnp.concatenate(
        [padded[:, shift : shift + row_patches] for shift in range(3)], axis=2
    ).transpose(1, 0, 2)
    spread, by_depth[1], by_depth[7] = barrier((spread, by_depth[1], by_depth[7]))
    near = exchange(spread).reshape(members, 3 * SLOTS)

    outgoing = turned(turned_fields, FIRST)
    outgoing, near, by_depth[2], by_depth[4], by_depth[6] = barrier(
        (outgoing, near, by_depth[2], by_depth[4], by_depth[6])
    )
    near = passed(near)
    near, by_depth[3], by_depth[5] = barrier((near, by_depth[3], by_depth[5]))
    incoming = exchange(outgoing)
    by_turn = gathered(by_depth)
    by_turn = [shifted(by_turn[turn - 1], turn, 0) for turn in range(1, TURNS)]

    pair_rows = jnp.pad(tables[:, OWN_BLOCKS:], ((1, 1), (0, 0), (0, 0)))
    pair_own = lax.dynamic_slice_in_dim(pair_rows, here, 3, axis=0)
    pair_above, pair_below = row_halo(pair_own)
    near_above, near_below = row_halo(near)
    nears = [near_above, near, near_below]
    weights, sided = weights_for(
        listed_blocks[0, 0],
        place,
        nears,
        [swapped(cells) for cells in nears],
        [pair_above, pair_own, pair_below],
    )
    outs = apply_first(sided, by_depth, by_turn, VARIABLES)
    incoming, outs = barrier((incoming, outs))
    outs = apply_rest(weights, incoming, outs)
    whole = turned(exchange(outs), params=SMALL)
    return whole.transpose(0, 2, 1, 3).reshape(ensemble.shape)


def solution(mesh):
    placed = (
        P("member", "patch", None, "level", None, None),
        P("patch", "member", None, None),
        P("patch", "member", None, None),
        P("patch", "member", None),
        P("patch", "member", None, None),
        P("level", None),
        P("patch", "member", None),
    )
    return jax.shard_map(
        body,
        mesh=mesh,
        in_specs=placed,
        out_specs=P("member", "patch", None, "level", None, None),
        check_vma=False,
    )
```

```python
import jax
import jax.numpy as jnp
from jax import lax
from jax.experimental import pallas as pl
from jax.experimental.pallas import tpu as pltpu
from jax.sharding import PartitionSpec as P

VARIABLES = 12
COLUMNS = 1024
SLOTS = 128
OWN_BLOCKS = 2
LISTED = 8
SWEEPS = 6
FIRST = 6
STEP = 3
PAIR = 3
DEPTHS = 8
TURNS = 4

exact_precision = lax.Precision.HIGHEST
barrier = lax.optimization_barrier


def exchange(cells):
    return lax.all_to_all(cells, "member", split_axis=0, concat_axis=0, tiled=True)


def row_halo(cells):
    count = lax.axis_size("patch")
    above = lax.ppermute(cells, "patch", [(i, i + 1) for i in range(count - 1)])
    below = lax.ppermute(cells, "patch", [(i + 1, i) for i in range(count - 1)])
    return above, below


def shifted(cells, turn, depth):
    pairs = []
    for y in range(TURNS):
        for z in range(DEPTHS):
            pairs.append((y * DEPTHS + z, (y + turn) % TURNS * DEPTHS + (z + depth) % DEPTHS))
    return lax.ppermute(cells, "member", pairs)


def swapped(cells):
    return lax.ppermute(cells, "level", [(0, 1), (1, 0)])


def cost(values, flops=0):
    return pl.CostEstimate(flops=flops, bytes_accessed=4 * values, transcendentals=0)


WEIGHTS_COST = pl.CostEstimate(flops=0, bytes_accessed=1024, transcendentals=0)
PARAMS = pltpu.CompilerParams(vmem_limit_bytes=56 * 1024 * 1024)
SMALL = pltpu.CompilerParams(vmem_limit_bytes=32 * 1024 * 1024)


def weights_kernel(listed_ref, place_ref, *refs):
    own_refs, other_refs, pair_refs = refs[:3], refs[3:6], refs[6:9]
    weights_ref, sided_ref, scaled_ref = refs[9:]
    members = own_refs[0].shape[0]
    total = jnp.zeros((members, SLOTS), jnp.float32)
    for j in range(LISTED):
        block = listed_ref[j]
        row = lax.div(block, 3 * OWN_BLOCKS)
        inside = lax.rem(block, 3 * OWN_BLOCKS)
        column = lax.div(inside, OWN_BLOCKS)
        which = lax.rem(inside, OWN_BLOCKS)
        away = jnp.abs(row - 1) + jnp.abs(column - 1)
        taper = jnp.where(away == 0, 1.0, jnp.where(away == 1, 0.6, 0.35)).astype(jnp.float32)
        lanes = pl.ds(pl.multiple_of(column * SLOTS, SLOTS), SLOTS)
        near_refs = zip(own_refs, other_refs)
        wide = [
            jnp.where(
                which == place_ref[2],
                own_ref[:, lanes].astype(jnp.float32),
                other_ref[:, lanes].astype(jnp.float32),
            )
            for own_ref, other_ref in near_refs
        ]
        wide = jnp.where(row == 0, wide[0], jnp.where(row == 1, wide[1], wide[2]))
        pair = [ref[column] for ref in pair_refs]
        pair = jnp.where(row == 0, pair[0], jnp.where(row == 1, pair[1], pair[2]))
        observed = jnp.where(which == 0, pair[0:1], pair[1:2])
        weight = jnp.where(which == 0, pair[2:3], pair[3:4]) * taper
        centre = jnp.sum(wide, axis=0, keepdims=True) * (1.0 / members)
        pert = (wide - centre).astype(jnp.bfloat16).astype(jnp.float32)
        scaled_ref[:, j * SLOTS : (j + 1) * SLOTS] = (pert * jnp.sqrt(weight)).astype(jnp.bfloat16)
        total = total + pert * (weight * (observed - centre))
    forcing = jnp.sum(total, axis=1, keepdims=True)
    scaled = scaled_ref[...]
    system = lax.dot_general(
        scaled, scaled, (((1,), (1,)), ((), ())), preferred_element_type=jnp.float32
    )
    rows = lax.broadcasted_iota(jnp.int32, (members, members), 0)
    columns = lax.broadcasted_iota(jnp.int32, (members, members), 1)
    identity = jnp.where(rows == columns, 1.0, 0.0).astype(jnp.float32)
    system = system + (members - 1) / 1.1 * identity
    scaling = jnp.sqrt(
        jnp.sum(jnp.sum(system * system, axis=1, keepdims=True), axis=0, keepdims=True)
    )
    iterate = system / scaling
    inverse_root = 1.5 * identity - 0.5 * iterate
    iterate = jnp.dot(iterate, inverse_root, precision=exact_precision)
    for iteration in range(1, SWEEPS):
        middle = 1.5 * identity - 0.5 * jnp.dot(inverse_root, iterate, precision=exact_precision)
        if iteration < SWEEPS - 1:
            iterate = jnp.dot(iterate, middle, precision=exact_precision)
        inverse_root = jnp.dot(middle, inverse_root, precision=exact_precision)
    forcing = jnp.broadcast_to(forcing, (members, SLOTS))
    inner = jnp.dot(inverse_root, forcing, precision=exact_precision)
    mean_weight = jnp.dot(inverse_root, inner, precision=exact_precision)[:, :1] / scaling
    weights = jnp.sqrt((members - 1) / scaling) * inverse_root + mean_weight
    weights = weights.T.astype(jnp.bfloat16)
    weights_ref[...] = weights

    own = members // (TURNS * DEPTHS)
    group = rows // own
    source_y = lax.rem(place_ref[0] + TURNS - group // DEPTHS, TURNS)
    source_z = lax.rem(place_ref[1] + DEPTHS - lax.rem(group, DEPTHS), DEPTHS)
    source = (source_y * DEPTHS + source_z) * own + lax.rem(rows, own)
    reorder = jnp.where(source == columns, 1.0, 0.0).astype(jnp.bfloat16)
    sided = lax.dot_general(
        weights, reorder, (((1,), (1,)), ((), ())), preferred_element_type=jnp.float32
    )
    sided_ref[...] = sided.astype(jnp.bfloat16)


def weights_for(listed, place, nears, others, pairs):
    members = nears[0].shape[0]
    vmem = pl.BlockSpec(memory_space=pltpu.VMEM)
    smem = pl.BlockSpec(memory_space=pltpu.SMEM)
    return pl.pallas_call(
        weights_kernel,
        in_specs=[smem, smem] + [vmem] * 9,
        out_specs=[vmem] * 2,
        out_shape=[jax.ShapeDtypeStruct((members, members), jnp.bfloat16)] * 2,
        scratch_shapes=[pltpu.VMEM((members, LISTED * SLOTS), jnp.bfloat16)],
        compiler_params=PARAMS,
        cost_estimate=WEIGHTS_COST,
    )(listed, place, *nears, *others, *pairs)


def patch_at(place_ref, turn, depth):
    y = lax.rem(place_ref[0] + turn, TURNS)
    z = lax.rem(place_ref[1] + depth, DEPTHS)
    return y * DEPTHS + z


def pack_first_kernel(place_ref, fields_ref, *refs):
    out_refs, scratch = refs[:-1], refs[-1]
    for level in range(PAIR):
        scratch[...] = jnp.swapaxes(fields_ref[:, level], 0, 1)
        for depth in range(DEPTHS):
            for turn in range(TURNS):
                out_refs[depth][turn, level] = scratch[patch_at(place_ref, turn, depth)]


def pack_first(place, fields, count):
    own, _, patches, columns = fields.shape
    return pl.pallas_call(
        pack_first_kernel,
        grid_spec=pltpu.PrefetchScalarGridSpec(
            num_scalar_prefetch=1,
            grid=(count // PAIR,),
            in_specs=[pl.BlockSpec((own, PAIR, patches, columns), lambda v, s: (0, v, 0, 0))],
            out_specs=[
                pl.BlockSpec((TURNS, PAIR, own, columns), lambda v, s: (0, v, 0, 0))
                for _ in range(DEPTHS)
            ],
            scratch_shapes=[pltpu.VMEM((patches, own, columns), fields.dtype)],
        ),
        out_shape=[
            jax.ShapeDtypeStruct((TURNS, count, own, columns), fields.dtype) for _ in range(DEPTHS)
        ],
        compiler_params=PARAMS,
        cost_estimate=cost(own * count * patches * columns),
    )(place, fields)


def table_kernel(count_ref, position_ref, observed_ref, precision_ref, out_ref):
    slot = lax.broadcasted_iota(jnp.int32, (1, SLOTS), 1)
    used = [
        jnp.where(slot < count_ref[block], precision_ref[block : block + 1], 0.0)
        for block in range(OWN_BLOCKS)
    ]
    table = jnp.concatenate(
        [position_ref[...].astype(jnp.float32), observed_ref[...]] + used, axis=0
    )
    out_ref[...] = jnp.broadcast_to(table[None], out_ref.shape)


def table_of(count, position, observed, precision, patches):
    vmem = pl.BlockSpec(memory_space=pltpu.VMEM)
    return pl.pallas_call(
        table_kernel,
        in_specs=[pl.BlockSpec(memory_space=pltpu.SMEM)] + [vmem] * 3,
        out_specs=vmem,
        out_shape=jax.ShapeDtypeStruct((patches, 3 * OWN_BLOCKS, SLOTS), jnp.float32),
    )(count, position, observed, precision)


def turn_kernel(fields_ref, out_ref):
    for level in range(fields_ref.shape[1]):
        out_ref[:, level] = jnp.swapaxes(fields_ref[:, level], 0, 1)


def turned(fields, low=0, params=PARAMS):
    outer, levels, inner, columns = fields.shape
    levels = levels - low
    return pl.pallas_call(
        turn_kernel,
        grid=(levels // STEP,),
        in_specs=[pl.BlockSpec((outer, STEP, inner, columns), lambda v: (0, v + low // STEP, 0, 0))],
        out_specs=pl.BlockSpec((inner, STEP, outer, columns), lambda v: (0, v, 0, 0)),
        out_shape=jax.ShapeDtypeStruct((inner, levels, outer, columns), fields.dtype),
        compiler_params=params,
        cost_estimate=cost(fields.size),
    )(fields)


def gather_kernel(*refs):
    by_depth, by_turn = refs[:DEPTHS], refs[DEPTHS:]
    for turn in range(1, TURNS):
        for depth in range(DEPTHS):
            by_turn[turn - 1][depth] = by_depth[depth][turn]


def gathered(by_depth):
    turns, count, own, columns = by_depth[0].shape
    return pl.pallas_call(
        gather_kernel,
        grid=(count // PAIR,),
        in_specs=[pl.BlockSpec((turns, PAIR, own, columns), lambda v: (0, v, 0, 0))] * DEPTHS,
        out_specs=[pl.BlockSpec((DEPTHS, PAIR, own, columns), lambda v: (0, v, 0, 0))] * (turns - 1),
        out_shape=[
            jax.ShapeDtypeStruct((DEPTHS, count, own, columns), by_depth[0].dtype)
            for _ in range(turns - 1)
        ],
        compiler_params=PARAMS,
        cost_estimate=pl.CostEstimate(flops=0, bytes_accessed=1 << 22, transcendentals=0),
    )(*by_depth)


def passed_kernel(cells_ref, out_ref):
    out_ref[...] = cells_ref[...]


def passed(cells):
    vmem = pl.BlockSpec(memory_space=pltpu.VMEM)
    return pl.pallas_call(
        passed_kernel,
        in_specs=[vmem],
        out_specs=vmem,
        out_shape=jax.ShapeDtypeStruct(cells.shape, cells.dtype),
        compiler_params=PARAMS,
        cost_estimate=pl.CostEstimate(flops=1 << 40, bytes_accessed=1 << 31, transcendentals=0),
    )(cells)


def analyse(weights, wide):
    mean = jnp.sum(wide, axis=0, keepdims=True) * (1.0 / wide.shape[0])
    pert = (wide - mean).astype(jnp.bfloat16)
    return jnp.dot(weights, pert, preferred_element_type=jnp.float32) + mean


def apply_first_kernel(weights_ref, *refs):
    by_depth, by_turn, out_ref = refs[:DEPTHS], refs[DEPTHS:-1], refs[-1]
    own, columns = by_depth[0].shape[2:]
    for level in range(PAIR):
        parts = [ref[0, level].astype(jnp.float32) for ref in by_depth]
        for ref in by_turn:
            parts.append(ref[:, level].astype(jnp.float32).reshape(DEPTHS * own, columns))
        updated = analyse(weights_ref[...], jnp.concatenate(parts, axis=0))
        updated = updated.reshape(TURNS * DEPTHS, own, columns)
        out_ref[:, level] = updated.astype(out_ref.dtype)


def apply_first(weights, by_depth, by_turn, levels):
    _, count, own, columns = by_depth[0].shape
    members = weights.shape[0]
    groups = TURNS * DEPTHS
    return pl.pallas_call(
        apply_first_kernel,
        grid=(count // PAIR,),
        in_specs=[pl.BlockSpec((members, members), lambda v: (0, 0))]
        + [pl.BlockSpec((1, PAIR, own, columns), lambda v: (0, v, 0, 0))] * DEPTHS
        + [pl.BlockSpec((DEPTHS, PAIR, own, columns), lambda v: (0, v, 0, 0))] * (TURNS - 1),
        out_specs=pl.BlockSpec((groups, PAIR, own, columns), lambda v: (0, v, 0, 0)),
        out_shape=jax.ShapeDtypeStruct((groups, levels, own, columns), jnp.bfloat16),
        compiler_params=PARAMS,
        cost_estimate=cost(members * count * columns, 2 * members * members * count * columns),
    )(weights, *by_depth, *by_turn)


def apply_rest_kernel(weights_ref, fields_ref, _, out_ref):
    sources, levels, own, columns = fields_ref.shape
    for level in range(levels):
        wide = fields_ref[:, level].astype(jnp.float32).reshape(sources * own, columns)
        updated = analyse(weights_ref[...], wide).reshape(sources, own, columns)
        out_ref[:, level] = updated.astype(out_ref.dtype)


def apply_rest(weights, fields, whole):
    sources, levels, own, columns = fields.shape
    members = weights.shape[0]
    low = whole.shape[1] - levels
    return pl.pallas_call(
        apply_rest_kernel,
        grid=(levels // STEP,),
        in_specs=[
            pl.BlockSpec((members, members), lambda v: (0, 0)),
            pl.BlockSpec((sources, STEP, own, columns), lambda v: (0, v, 0, 0)),
            pl.BlockSpec(memory_space=pl.ANY),
        ],
        out_specs=pl.BlockSpec(
            (sources, STEP, own, columns), lambda v: (0, v + low // STEP, 0, 0)
        ),
        out_shape=jax.ShapeDtypeStruct(whole.shape, whole.dtype),
        input_output_aliases={2: 0},
        compiler_params=PARAMS,
        cost_estimate=cost(fields.size, 2 * members * fields.size),
    )(weights, fields, whole)


def observe(shaped_fields, where_flat, kernel):
    patch_count = where_flat.shape[0]
    slot_count = where_flat.shape[1]
    column_of = where_flat % COLUMNS
    variable_of = where_flat // COLUMNS
    column_iota = lax.broadcasted_iota(jnp.int32, (patch_count, COLUMNS, slot_count), 1)
    column_hot = (column_of[:, None, :] == column_iota).astype(jnp.bfloat16)
    spread = jnp.einsum(
        "kpvq,pqo->kpvo", shaped_fields, column_hot, preferred_element_type=jnp.float32
    )
    variable_iota = lax.broadcasted_iota(jnp.int32, (patch_count, VARIABLES, slot_count), 1)
    variable_weight = jnp.where(
        variable_of[:, None, :] == variable_iota, kernel[None, :, None], 0.0
    )
    return jnp.sum(spread * variable_weight[None], axis=2)


def body(ensemble, observations, precision, valid_count, position, level_kernel, listed_blocks):
    kernel = level_kernel[0]
    own = ensemble.shape[0]
    row_patches = ensemble.shape[2]
    members = own * row_patches
    fields = ensemble.reshape(own, row_patches, VARIABLES, COLUMNS)
    turned_fields = fields.transpose(0, 2, 1, 3)
    here = lax.axis_index("member")
    level = lax.axis_index("level")
    place = jnp.stack([here // DEPTHS, here % DEPTHS, level]).astype(jnp.int32)

    tables = exchange(
        table_of(
            valid_count.reshape(OWN_BLOCKS),
            position.reshape(OWN_BLOCKS, SLOTS),
            observations.reshape(OWN_BLOCKS, SLOTS),
            precision.reshape(OWN_BLOCKS, SLOTS),
            row_patches,
        )
    )

    packed = pack_first(place, turned_fields, FIRST)
    by_depth = [packed[0]] + [shifted(packed[depth], 0, depth) for depth in range(1, DEPTHS)]

    where = tables[:, :OWN_BLOCKS].reshape(row_patches, OWN_BLOCKS * SLOTS).astype(jnp.int32)
    level_term = observe(fields, where, kernel)
    equivalent = lax.psum(level_term, "level").astype(jnp.bfloat16)
    equivalent = jnp.where(level == 0, equivalent[:, :, :SLOTS], equivalent[:, :, SLOTS:])
    padded = jnp.pad(equivalent, ((0, 0), (1, 1), (0, 0)))
    spread = jnp.concatenate(
        [padded[:, shift : shift + row_patches] for shift in range(3)], axis=2
    ).transpose(1, 0, 2)
    spread, by_depth[1], by_depth[7] = barrier((spread, by_depth[1], by_depth[7]))
    near = exchange(spread).reshape(members, 3 * SLOTS)

    outgoing = turned(turned_fields, FIRST)
    outgoing, near, by_depth[2], by_depth[4], by_depth[6] = barrier(
        (outgoing, near, by_depth[2], by_depth[4], by_depth[6])
    )
    near = passed(near)
    near, by_depth[3], by_depth[5] = barrier((near, by_depth[3], by_depth[5]))
    incoming = exchange(outgoing)
    by_turn = gathered(by_depth)
    by_turn = [shifted(by_turn[turn - 1], turn, 0) for turn in range(1, TURNS)]

    pair_rows = jnp.pad(tables[:, OWN_BLOCKS:], ((1, 1), (0, 0), (0, 0)))
    pair_own = lax.dynamic_slice_in_dim(pair_rows, here, 3, axis=0)
    pair_above, pair_below = row_halo(pair_own)
    near_above, near_below = row_halo(near)
    nears = [near_above, near, near_below]
    weights, sided = weights_for(
        listed_blocks[0, 0],
        place,
        nears,
        [swapped(cells) for cells in nears],
        [pair_above, pair_own, pair_below],
    )
    outs = apply_first(sided, by_depth, by_turn, VARIABLES)
    incoming, outs = barrier((incoming, outs))
    outs = apply_rest(weights, incoming, outs)
    whole = turned(exchange(outs), params=SMALL)
    return whole.transpose(0, 2, 1, 3).reshape(ensemble.shape)


def solution(mesh):
    placed = (
        P("member", "patch", None, "level", None, None),
        P("patch", "member", None, None),
        P("patch", "member", None, None),
        P("patch", "member", None),
        P("patch", "member", None, None),
        P("level", None),
        P("patch", "member", None),
    )
    return jax.shard_map(
        body,
        mesh=mesh,
        in_specs=placed,
        out_specs=P("member", "patch", None, "level", None, None),
        check_vma=False,
    )
```
